32 devices in a mesh: parts: 2 (over x), wide: 8 (over z, y), loop: 2 (over core).
Axes of the slice: x: 2, y: 2, z: 4, core: 2. Of those that a mesh axis runs over, the one named last changes fastest.
Arguments:
- density: bfloat16 [37, 32768], P(None, ('parts', 'wide', 'loop')), parts along dimension 1, may hold values from -6 to 6
- near_blocks: bfloat16 [128, 8, 256, 256], P(('parts', 'wide', 'loop')), parts along dimension 0, may hold values from -0.125 to 0.125
- near_source: int32 [128, 8], P(('parts', 'wide', 'loop')), parts along dimension 0, may hold values from 0 to 7
- source_basis: bfloat16 [128, 64, 256], P(('parts', 'wide', 'loop')), parts along dimension 0, may hold values from -0.375 to 0.375
- cluster_of: int32 [128], P(('parts', 'wide', 'loop')), parts along dimension 0, may hold values from 0 to 1
- translation: bfloat16 [4096, 2048], P(('parts', 'wide', 'loop')), parts along dimension 0, may hold values from -0.125 to 0.125
- eval_basis: bfloat16 [128, 64, 256], P(('parts', 'wide', 'loop')), parts along dimension 0, may hold values from -0.75 to 0.75
Outputs:
- powers: bfloat16 [4, 37, 32768], P(None, None, ('parts', 'wide', 'loop')), parts along dimension 2
The draws below stay inside these ranges and needn't reach their ends.
There are 2 independent parts, one for each index of `parts`. The reference program is written for one: setup_inputs(seed, part) draws one part's arguments, and reference() takes and returns one part's arrays. A program takes and returns all parts, laid end to end along the dimension named above; each array names one. Nothing has to cross between parts.
All inputs are finite; a program needn't handle non-finite values.
Results may differ from the reference program's by a relative error of at most 0.011.
Values may be sent and summed in bfloat16 or wider, within the bound.
A program may use at most 64 MiB of HBM per device.

```python
import jax
import jax.numpy as jnp
from jax import lax

K = 37
B = 256
R = 64
NB = 8
CL_DEV = 2
APPLIES = 4
PAN_DEV = 4
PANELS = 64
NC = 32
N = 16384
N_LOOP = 2


def touch_ends(entries, rng, smallest, top_value):
    extent = entries.shape
    spot = [jax.random.randint(jax.random.fold_in(rng, axis), (), 0, extent[axis]) for axis in range(len(extent))]
    entries = entries.at[tuple(spot)].set(smallest)
    longest = extent.index(max(extent))
    spot[longest] = (spot[longest] + 1) % extent[longest]
    return entries.at[tuple(spot)].set(top_value)


def levels(stream_key, dims, shards, smallest, largest):
    def one(axis_at, parts):
        draws = jax.random.uniform(jax.random.fold_in(jax.random.fold_in(stream_key, 6), axis_at), (parts,), jnp.float32, smallest / len(shards), largest / len(shards))
        return jnp.repeat(jnp.exp(draws), dims[axis_at] // parts).reshape((-1,) + (1,) * (len(dims) - axis_at - 1))

    level = one(*shards[0])
    for cut in shards[1:]:
        level = level * one(*cut)
    return level


def bell_draw(own_key, shape, scale, most, split=(), dtype=jnp.bfloat16):
    level = levels(own_key, shape, split, -0.22, 0.18) if split else 1.0
    entries = jax.random.normal(own_key, shape, jnp.float32) * scale * level
    return jnp.minimum(jnp.maximum(entries, -most), most).astype(dtype)


def setup_inputs(seed: int = 0, part: int = 0) -> dict:
    key_list = jax.random.split(jax.random.key(seed), 8)
    part_splits = jax.random.split(jax.random.fold_in(key_list[7], part), 8)
    density = bell_draw(part_splits[0], (K, N), 1.0, 6.0, ((1, 16),))
    near_blocks = bell_draw(part_splits[1], (PANELS, NB, B, B), (NB * B) ** -0.5, 0.125, ((0, 16),))
    near_source = touch_ends(jax.random.randint(part_splits[2], (PANELS, NB), 0, N_LOOP * PAN_DEV), jax.random.fold_in(part_splits[2], 1), 0, (N_LOOP * PAN_DEV) - 1).astype(jnp.int32)
    source_basis = bell_draw(part_splits[3], (PANELS, R, B), B ** -0.5, 0.375, ((0, 16),))
    cluster_of = touch_ends(jax.random.randint(part_splits[4], (PANELS,), 0, CL_DEV), jax.random.fold_in(part_splits[4], 1), 0, CL_DEV - 1).astype(jnp.int32)
    translation = bell_draw(part_splits[5], (NC * R, NC * R), (NC * R) ** -0.5, 0.125, ((0, 16),))
    eval_basis = bell_draw(part_splits[6], (PANELS, R, B), R ** -0.5, 0.75, ((0, 16),))
    return dict(density=density, near_blocks=near_blocks, near_source=near_source, source_basis=source_basis, cluster_of=cluster_of, translation=translation, eval_basis=eval_basis)


def near_panel(pair):
    selected, blocks = pair
    return jnp.einsum('knb,nab->ka', selected.astype(jnp.float32), blocks.astype(jnp.float32))


def apply_operator(field, near_blocks, near_source, source_basis, cluster_of, translation, eval_basis):
    panels = field.reshape(K, PANELS, B)
    span = N_LOOP * PAN_DEV
    group = (jnp.arange(PANELS) // span).astype(jnp.int32)
    sources = (group[:, None] * span + near_source).astype(jnp.int32)
    selected = jnp.moveaxis(panels[:, sources, :], 1, 0)
    near = jnp.moveaxis(lax.map(near_panel, (selected, near_blocks)), 0, 1)
    coefficients = jnp.einsum('kpb,prb->kpr', panels.astype(jnp.float32), source_basis.astype(jnp.float32))
    cluster = ((jnp.arange(PANELS) // PAN_DEV) * CL_DEV + cluster_of).astype(jnp.int32)
    summed = jax.ops.segment_sum(jnp.moveaxis(coefficients, 1, 0), cluster, num_segments=NC)
    cluster_coeffs = jnp.moveaxis(summed, 0, 1).astype(jnp.bfloat16).reshape(K, NC * R)
    expansion = lax.dot_general(cluster_coeffs, translation, (((1,), (1,)), ((), ())), preferred_element_type=jnp.float32)
    expansion = expansion.astype(jnp.bfloat16).reshape(K, NC, R)
    picked = expansion[:, cluster, :]
    far = jnp.einsum('kpr,pra->kpa', picked.astype(jnp.float32), eval_basis.astype(jnp.float32))
    return (near + far).astype(jnp.bfloat16).reshape(K, N)


def reference(density, near_blocks, near_source, source_basis, cluster_of, translation, eval_basis):
    current = density
    results = []
    for number in range(APPLIES):
        current = apply_operator(current, near_blocks, near_source, source_basis, cluster_of, translation, eval_basis)
        results.append(current)
    return jnp.stack(results, axis=0)
```

```python
import functools

import jax
import jax.numpy as jnp
from jax import lax
from jax.experimental import pallas as pl
from jax.experimental.pallas import tpu as pltpu
from jax.sharding import PartitionSpec as P

CL_DEV = 2
APPLIES = 4
MESH = pl.DeviceIdType.MESH
NT = (((1,), (1,)), ((), ()))


def dot_nt(a, b):
    return lax.dot_general(a, b, NT, preferred_element_type=jnp.float32)


def kernel(
    wides, loops, count,
    clusters, sources, density, near_hbm, source_hbm, translation_hbm, eval_hbm,
    out,
    field0, field1, field2, field3, gathered, near_vmem, source_vmem, translation_vmem,
    eval_vmem, source_all, eval_all, near_sum,
    load_sem, field_send, field_recv, block_send, block_recv, pass_send, pass_recv,
):
    fields = (field0, field1, field2, field3)
    wide = lax.axis_index("wide")
    loop = lax.axis_index("loop")
    other = 1 - loop
    rows = density.shape[0]
    padded, elements = field0.shape[1:]
    near_count = sources.shape[1]
    rank = source_hbm.shape[1]
    width = CL_DEV * rank

    def peer(step):
        return lax.rem(wide + step, wides)

    loads = [
        pltpu.make_async_copy(source_hbm, source_vmem, load_sem.at[0]),
        pltpu.make_async_copy(eval_hbm, eval_vmem, load_sem.at[1]),
        pltpu.make_async_copy(near_hbm, near_vmem, load_sem.at[2]),
        pltpu.make_async_copy(translation_hbm, translation_vmem, load_sem.at[3]),
    ]
    for load in loads:
        load.start()

    barrier = pltpu.get_barrier_semaphore()
    pl.semaphore_signal(barrier, inc=1, device_id={"loop": other}, device_id_type=MESH)

    def greet(step, carry):
        pl.semaphore_signal(
            barrier, inc=1, device_id={"wide": peer(step)}, device_id_type=MESH
        )
        return carry

    lax.fori_loop(1, wides, greet, 0)

    mine = loop * count
    for p in range(count):
        field0[mine + p] = jnp.zeros((padded, elements), jnp.bfloat16)
        field0[mine + p, 0:rows, :] = density[:, p * elements : (p + 1) * elements]
    loads[0].wait()
    loads[1].wait()
    for p in range(count):
        for c in range(CL_DEV):
            chosen = clusters[0, p] == c
            source_all[c * rank : (c + 1) * rank, p * elements : (p + 1) * elements] = jnp.where(
                chosen, source_vmem[p], jnp.zeros((rank, elements), jnp.bfloat16)
            )
            eval_all[c * rank : (c + 1) * rank, p * elements : (p + 1) * elements] = jnp.where(
                chosen, eval_vmem[p], jnp.zeros((rank, elements), jnp.bfloat16)
            )
    pl.semaphore_wait(barrier, wides)

    def field_copy(j):
        part = fields[j].at[pl.ds(mine, count)]
        return pltpu.make_async_remote_copy(
            src_ref=part, dst_ref=part, send_sem=field_send.at[j], recv_sem=field_recv.at[j],
            device_id={"loop": other}, device_id_type=MESH,
        )

    def block_copy(j, step):
        block = gathered.at[j, loop, wide]
        return pltpu.make_async_remote_copy(
            src_ref=block, dst_ref=block, send_sem=block_send.at[j], recv_sem=block_recv.at[j, step],
            device_id={"wide": peer(step)}, device_id_type=MESH,
        )

    def arrived(j, step):
        block = gathered.at[j, loop, lax.rem(wide - step + wides, wides)]
        return pltpu.make_async_remote_copy(
            src_ref=block, dst_ref=block, send_sem=block_send.at[j], recv_sem=block_recv.at[j, step],
            device_id={"wide": peer(step)}, device_id_type=MESH,
        )

    def pass_copy(j, step):
        block = gathered.at[j, loop, lax.rem(wide - step + wides, wides)]
        return pltpu.make_async_remote_copy(
            src_ref=block, dst_ref=block, send_sem=pass_send.at[j], recv_sem=pass_recv.at[j],
            device_id={"loop": other}, device_id_type=MESH,
        )

    def each(first, last, body):
        if wides <= 8:
            for step in range(first, last):
                body(step)
        else:
            lax.fori_loop(first, last, lambda step, carry: (body(step), carry)[1], 0)

    for j in range(APPLIES):
        field = fields[j]
        field_copy(j).start()
        own = jnp.concatenate([field[mine + p] for p in range(count)], axis=1)
        gathered[j, loop, wide] = dot_nt(own, source_all[...]).astype(jnp.bfloat16)

        def send(step):
            block_copy(j, step).start()

        each(1, wides, send)
        pass_copy(j, 0).start()

        field_copy(j).wait_recv()
        if j == 0:
            loads[2].wait()
        for p in range(count):
            total = None
            for n in range(near_count):
                term = dot_nt(field[sources[p, n]], near_vmem[p, n])
                total = term if total is None else total + term
            near_sum[p] = total

        def forward(step):
            arrived(j, step).wait_recv()
            pass_copy(j, step).start()

        each(1, wides, forward)
        if j == 0:
            loads[3].wait()
        whole = gathered.at[j, other]
        pltpu.make_async_remote_copy(
            src_ref=whole, dst_ref=whole, send_sem=pass_send.at[j], recv_sem=pass_recv.at[j],
            device_id={"loop": other}, device_id_type=MESH,
        ).wait_recv()
        total = None
        chunk = 8
        for start in range(0, wides, chunk):
            here = range(start, min(start + chunk, wides))
            blocks = [gathered[j, l, w] for w in here for l in range(loops)]
            columns = slice(start * loops * width, (here[-1] + 1) * loops * width)
            term = dot_nt(jnp.concatenate(blocks, axis=1), translation_vmem[:, columns])
            total = term if total is None else total + term
        expansion = total.astype(jnp.bfloat16)
        for p in range(count):
            far = jnp.dot(
                expansion, eval_all[:, p * elements : (p + 1) * elements],
                preferred_element_type=jnp.float32,
            )
            value = (near_sum[p] + far).astype(jnp.bfloat16)
            if j + 1 < APPLIES:
                fields[j + 1][mine + p] = value
            out[j, :, p * elements : (p + 1) * elements] = value[:rows]

    for j in range(APPLIES):
        field_copy(j).wait_send()
        every = gathered.at[j, loop]
        most = gathered.at[j, loop, pl.ds(0, wides - 1)]
        for ref, sem in ((every, pass_send), (most, block_send)):
            pltpu.make_async_remote_copy(
                src_ref=ref, dst_ref=ref, send_sem=sem.at[j], recv_sem=pass_recv.at[j],
                device_id={"loop": other}, device_id_type=MESH,
            ).wait_send()


def per_device(
    density, near_blocks, near_source, source_basis, cluster_of, translation, eval_basis
):
    wides, loops = lax.axis_size("wide"), lax.axis_size("loop")
    rows, size = density.shape
    count, near_count, elements, _ = near_blocks.shape
    rank = source_basis.shape[1]
    width = CL_DEV * rank
    padded = -(-rows // 16) * 16
    vmem = pl.BlockSpec(memory_space=pltpu.VMEM)
    smem = pl.BlockSpec(memory_space=pltpu.SMEM)
    anywhere = pl.BlockSpec(memory_space=pl.ANY)
    low, full = jnp.bfloat16, jnp.float32
    return pl.pallas_call(
        functools.partial(kernel, wides, loops, count),
        out_shape=jax.ShapeDtypeStruct((APPLIES, rows, size), low),
        in_specs=[smem, smem, vmem, anywhere, anywhere, anywhere, anywhere],
        out_specs=vmem,
        scratch_shapes=[pltpu.VMEM((loops * count, padded, elements), low)] * APPLIES
        + [
            pltpu.VMEM((APPLIES, loops, wides, padded, width), low),
            pltpu.VMEM(near_blocks.shape, low),
            pltpu.VMEM(source_basis.shape, low),
            pltpu.VMEM(translation.shape, low),
            pltpu.VMEM(eval_basis.shape, low),
            pltpu.VMEM((width, size), low),
            pltpu.VMEM((width, size), low),
            pltpu.VMEM((count, padded, elements), full),
            pltpu.SemaphoreType.DMA((4,)),
            pltpu.SemaphoreType.DMA((APPLIES,)),
            pltpu.SemaphoreType.DMA((APPLIES,)),
            pltpu.SemaphoreType.DMA((APPLIES,)),
            pltpu.SemaphoreType.DMA((APPLIES, wides)),
            pltpu.SemaphoreType.DMA((APPLIES,)),
            pltpu.SemaphoreType.DMA((APPLIES,)),
        ],
        compiler_params=pltpu.CompilerParams(
            collective_id=0, has_side_effects=True, vmem_limit_bytes=40 * 2**20
        ),
        name="apply_operator",
    )(
        cluster_of.reshape(1, count), near_source, density, near_blocks, source_basis,
        translation, eval_basis,
    )


def solution(mesh):
    split = ("parts", "wide", "loop")
    return jax.shard_map(
        per_device,
        mesh=mesh,
        in_specs=(
            P(None, split),
            P(split, None, None, None),
            P(split, None),
            P(split, None, None),
            P(split),
            P(split, None),
            P(split, None, None),
        ),
        out_specs=P(None, None, split),
        check_vma=False,
    )
```

```python
import functools

import jax
import jax.numpy as jnp
from jax import lax
from jax.experimental import pallas as pl
from jax.experimental.pallas import tpu as pltpu
from jax.sharding import PartitionSpec as P

CL_DEV = 2
APPLIES = 4
MESH = pl.DeviceIdType.MESH
NT = (((1,), (1,)), ((), ()))


def dot_nt(a, b):
    return lax.dot_general(a, b, NT, preferred_element_type=jnp.float32)


def kernel(
    wides, loops, count,
    clusters_hbm, sources_hbm, density_hbm, near_hbm, source_hbm, translation_hbm, eval_hbm,
    out,
    field0, field1, field2, field3, gathered, near_vmem, source_vmem, translation_vmem,
    eval_vmem, density, clusters, sources, source_all, eval_all, near_sum,
    load_sem, field_send, field_recv, block_send, block_recv, pass_send, pass_recv,
):
    fields = (field0, field1, field2, field3)
    wide = lax.axis_index("wide")
    loop = lax.axis_index("loop")
    other = 1 - loop
    rows = density.shape[0]
    padded, elements = field0.shape[1:]
    near_count = sources.shape[1]
    rank = source_hbm.shape[1]
    width = CL_DEV * rank

    def peer(step):
        return lax.rem(wide + step, wides)

    loads = [
        pltpu.make_async_copy(source_hbm, source_vmem, load_sem.at[0]),
        pltpu.make_async_copy(eval_hbm, eval_vmem, load_sem.at[1]),
        pltpu.make_async_copy(near_hbm, near_vmem, load_sem.at[2]),
        pltpu.make_async_copy(translation_hbm, translation_vmem, load_sem.at[3]),
        pltpu.make_async_copy(density_hbm, density, load_sem.at[4]),
        pltpu.make_async_copy(clusters_hbm, clusters, load_sem.at[5]),
        pltpu.make_async_copy(sources_hbm, sources, load_sem.at[6]),
    ]
    for number in (4, 0, 5, 6, 1, 2, 3):
        loads[number].start()

    barrier = pltpu.get_barrier_semaphore()
    pl.semaphore_signal(barrier, inc=1, device_id={"loop": other}, device_id_type=MESH)

    def greet(step, carry):
        pl.semaphore_signal(
            barrier, inc=1, device_id={"wide": peer(step)}, device_id_type=MESH
        )
        return carry

    lax.fori_loop(1, wides, greet, 0)

    mine = loop * count
    loads[4].wait()
    for p in range(count):
        field0[mine + p] = jnp.zeros((padded, elements), jnp.bfloat16)
        field0[mine + p, 0:rows, :] = density[:, p * elements : (p + 1) * elements]
    for number in (0, 5, 6, 1):
        loads[number].wait()
    for p in range(count):
        for c in range(CL_DEV):
            chosen = clusters[p] == c
            source_all[c * rank : (c + 1) * rank, p * elements : (p + 1) * elements] = jnp.where(
                chosen, source_vmem[p], jnp.zeros((rank, elements), jnp.bfloat16)
            )
            eval_all[c * rank : (c + 1) * rank, p * elements : (p + 1) * elements] = jnp.where(
                chosen, eval_vmem[p], jnp.zeros((rank, elements), jnp.bfloat16)
            )
    pl.semaphore_wait(barrier, wides)

    def field_copy(j):
        part = fields[j].at[pl.ds(mine, count)]
        return pltpu.make_async_remote_copy(
            src_ref=part, dst_ref=part, send_sem=field_send.at[j], recv_sem=field_recv.at[j],
            device_id={"loop": other}, device_id_type=MESH,
        )

    def block_copy(j, step):
        block = gathered.at[j, loop, wide]
        return pltpu.make_async_remote_copy(
            src_ref=block, dst_ref=block, send_sem=block_send.at[j], recv_sem=block_recv.at[j, step],
            device_id={"wide": peer(step)}, device_id_type=MESH,
        )

    def arrived(j, step):
        block = gathered.at[j, loop, lax.rem(wide - step + wides, wides)]
        return pltpu.make_async_remote_copy(
            src_ref=block, dst_ref=block, send_sem=block_send.at[j], recv_sem=block_recv.at[j, step],
            device_id={"wide": peer(step)}, device_id_type=MESH,
        )

    def pass_copy(j, step):
        block = gathered.at[j, loop, lax.rem(wide - step + wides, wides)]
        return pltpu.make_async_remote_copy(
            src_ref=block, dst_ref=block, send_sem=pass_send.at[j], recv_sem=pass_recv.at[j],
            device_id={"loop": other}, device_id_type=MESH,
        )

    def each(first, last, body):
        if wides <= 8:
            for step in range(first, last):
                body(step)
        else:
            lax.fori_loop(first, last, lambda step, carry: (body(step), carry)[1], 0)

    for j in range(APPLIES):
        field = fields[j]
        field_copy(j).start()
        own = jnp.concatenate([field[mine + p] for p in range(count)], axis=1)
        gathered[j, loop, wide] = dot_nt(own, source_all[...]).astype(jnp.bfloat16)

        def send(step):
            block_copy(j, step).start()

        each(1, wides, send)
        pass_copy(j, 0).start()

        field_copy(j).wait_recv()
        if j == 0:
            loads[2].wait()
        for p in range(count):
            total = None
            for n in range(near_count):
                term = dot_nt(field[sources[p, n]], near_vmem[p, n])
                total = term if total is None else total + term
            near_sum[p] = total

        def forward(step):
            arrived(j, step).wait_recv()
            pass_copy(j, step).start()

        each(1, wides, forward)
        if j == 0:
            loads[3].wait()
        whole = gathered.at[j, other]
        pltpu.make_async_remote_copy(
            src_ref=whole, dst_ref=whole, send_sem=pass_send.at[j], recv_sem=pass_recv.at[j],
            device_id={"loop": other}, device_id_type=MESH,
        ).wait_recv()
        total = None
        chunk = 8
        for start in range(0, wides, chunk):
            here = range(start, min(start + chunk, wides))
            blocks = [gathered[j, l, w] for w in here for l in range(loops)]
            columns = slice(start * loops * width, (here[-1] + 1) * loops * width)
            term = dot_nt(jnp.concatenate(blocks, axis=1), translation_vmem[:, columns])
            total = term if total is None else total + term
        expansion = total.astype(jnp.bfloat16)
        for p in range(count):
            far = jnp.dot(
                expansion, eval_all[:, p * elements : (p + 1) * elements],
                preferred_element_type=jnp.float32,
            )
            value = (near_sum[p] + far).astype(jnp.bfloat16)
            if j + 1 < APPLIES:
                fields[j + 1][mine + p] = value
            out[j, :, p * elements : (p + 1) * elements] = value[:rows]

    for j in range(APPLIES):
        field_copy(j).wait_send()
        every = gathered.at[j, loop]
        most = gathered.at[j, loop, pl.ds(0, wides - 1)]
        for ref, sem in ((every, pass_send), (most, block_send)):
            pltpu.make_async_remote_copy(
                src_ref=ref, dst_ref=ref, send_sem=sem.at[j], recv_sem=pass_recv.at[j],
                device_id={"loop": other}, device_id_type=MESH,
            ).wait_send()


def per_device(
    density, near_blocks, near_source, source_basis, cluster_of, translation, eval_basis
):
    wides, loops = lax.axis_size("wide"), lax.axis_size("loop")
    rows, size = density.shape
    count, near_count, elements, _ = near_blocks.shape
    rank = source_basis.shape[1]
    width = CL_DEV * rank
    padded = -(-rows // 16) * 16
    vmem = pl.BlockSpec(memory_space=pltpu.VMEM)
    anywhere = pl.BlockSpec(memory_space=pl.ANY)
    low, full = jnp.bfloat16, jnp.float32
    return pl.pallas_call(
        functools.partial(kernel, wides, loops, count),
        out_shape=jax.ShapeDtypeStruct((APPLIES, rows, size), low),
        in_specs=[anywhere] * 7,
        out_specs=vmem,
        scratch_shapes=[pltpu.VMEM((loops * count, padded, elements), low)] * APPLIES
        + [
            pltpu.VMEM((APPLIES, loops, wides, padded, width), low),
            pltpu.VMEM(near_blocks.shape, low),
            pltpu.VMEM(source_basis.shape, low),
            pltpu.VMEM(translation.shape, low),
            pltpu.VMEM(eval_basis.shape, low),
            pltpu.VMEM(density.shape, low),
            pltpu.SMEM(cluster_of.shape, jnp.int32),
            pltpu.SMEM(near_source.shape, jnp.int32),
            pltpu.VMEM((width, size), low),
            pltpu.VMEM((width, size), low),
            pltpu.VMEM((count, padded, elements), full),
            pltpu.SemaphoreType.DMA((7,)),
            pltpu.SemaphoreType.DMA((APPLIES,)),
            pltpu.SemaphoreType.DMA((APPLIES,)),
            pltpu.SemaphoreType.DMA((APPLIES,)),
            pltpu.SemaphoreType.DMA((APPLIES, wides)),
            pltpu.SemaphoreType.DMA((APPLIES,)),
            pltpu.SemaphoreType.DMA((APPLIES,)),
        ],
        compiler_params=pltpu.CompilerParams(
            collective_id=0, has_side_effects=True, vmem_limit_bytes=60 * 2**20
        ),
        name="apply_operator",
    )(
        cluster_of, near_source, density, near_blocks, source_basis,
        translation, eval_basis,
    )


def solution(mesh):
    split = ("parts", "wide", "loop")
    return jax.shard_map(
        per_device,
        mesh=mesh,
        in_specs=(
            P(None, split),
            P(split, None, None, None),
            P(split, None),
            P(split, None, None),
            P(split),
            P(split, None),
            P(split, None, None),
        ),
        out_specs=P(None, None, split),
        check_vma=False,
    )
```

```python
import functools

import jax
import jax.numpy as jnp
from jax import lax
from jax.experimental import pallas as pl
from jax.experimental.pallas import tpu as pltpu
from jax.sharding import PartitionSpec as P

CL_DEV = 2
APPLIES = 4
MESH = pl.DeviceIdType.MESH
NT = (((1,), (1,)), ((), ()))


def dot_nt(a, b):
    return lax.dot_general(a, b, NT, preferred_element_type=jnp.float32)


def kernel(
    wides, loops, count,
    clusters_hbm, sources_hbm, density_hbm, near_hbm, source_hbm, translation_hbm, eval_hbm,
    out,
    field0, field1, field2, field3, gathered, near_vmem, source_vmem, both,
    eval_vmem, density, clusters, sources, source_all, eval_all, near_sum,
    load_sem, field_send, field_recv, block_send, block_recv,
):
    fields = (field0, field1, field2, field3)
    wide = lax.axis_index("wide")
    loop = lax.axis_index("loop")
    other = 1 - loop
    rows = density.shape[0]
    padded, elements = field0.shape[1:]
    near_count = sources.shape[1]
    rank = source_hbm.shape[1]
    width = CL_DEV * rank
    pair = loops * width
    half = max(wides // 2, 1)
    paired = wides & (wides - 1) == 0

    def partner(step):
        flipped, bit = 0, 1
        while bit < wides:
            mine_bit, step_bit = wide // bit % 2, step // bit % 2
            flipped = flipped + bit * (mine_bit + step_bit - 2 * mine_bit * step_bit)
            bit *= 2
        return flipped

    def target(step):
        return partner(step) if paired else lax.rem(wide + step, wides)

    def origin(step):
        return partner(step) if paired else lax.rem(wide - step + wides, wides)

    def each(first, last, body):
        if last - first <= 8:
            for step in reversed(range(first, last)):
                body(step)
        else:
            lax.fori_loop(0, last - first, lambda i, carry: (body(last - 1 - i), carry)[1], 0)

    barrier = pltpu.get_barrier_semaphore()

    def greet(step):
        for l in (loop, other):
            pl.semaphore_signal(
                barrier, inc=1, device_id={"wide": target(step), "loop": l}, device_id_type=MESH
            )

    each(1, wides, greet)
    pl.semaphore_signal(barrier, inc=1, device_id={"loop": other}, device_id_type=MESH)

    loads = [
        pltpu.make_async_copy(source_hbm, source_vmem, load_sem.at[0]),
        pltpu.make_async_copy(eval_hbm, eval_vmem, load_sem.at[1]),
        pltpu.make_async_copy(near_hbm, near_vmem, load_sem.at[2]),
        pltpu.make_async_copy(translation_hbm, both.at[pl.ds(0, width)], load_sem.at[3]),
        pltpu.make_async_copy(density_hbm, density, load_sem.at[4]),
        pltpu.make_async_copy(clusters_hbm, clusters, load_sem.at[5]),
        pltpu.make_async_copy(sources_hbm, sources, load_sem.at[6]),
    ]
    for number in (4, 0, 5, 6, 1, 3, 2):
        loads[number].start()

    mine = loop * count
    loads[4].wait()
    for p in range(count):
        field0[mine + p] = jnp.zeros((padded, elements), jnp.bfloat16)
        field0[mine + p, 0:rows, :] = density[:, p * elements : (p + 1) * elements]
    for number in (0, 5, 6, 1):
        loads[number].wait()
    for p in range(count):
        for c in range(CL_DEV):
            chosen = clusters[p] == c
            source_all[c * rank : (c + 1) * rank, p * elements : (p + 1) * elements] = jnp.where(
                chosen, source_vmem[p], jnp.zeros((rank, elements), jnp.bfloat16)
            )
            eval_all[c * rank : (c + 1) * rank, p * elements : (p + 1) * elements] = jnp.where(
                chosen, eval_vmem[p], jnp.zeros((rank, elements), jnp.bfloat16)
            )
    own = jnp.concatenate([field0[mine + p] for p in range(count)], axis=1)
    gathered[0, loop] = dot_nt(own, source_all[...]).astype(jnp.bfloat16)

    def remote(ref, send, recv, device):
        return pltpu.make_async_remote_copy(
            src_ref=ref[0], dst_ref=ref[1], send_sem=send, recv_sem=recv,
            device_id=device, device_id_type=MESH,
        )

    def field_copy(j):
        part = fields[j].at[pl.ds(mine, count)]
        return remote((part, part), field_send.at[j], field_recv.at[j], {"loop": other})

    def send_blocks(j, first, last):
        def body(step):
            for l in (loop, other):
                remote(
                    (gathered.at[j, loop], gathered.at[j, loops * step + loop]),
                    block_send.at[j], block_recv.at[j, 0 if step_near(step) else 1],
                    {"wide": target(step), "loop": l},
                ).start()

        def step_near(step):
            return last <= half

        each(max(first, 1), last, body)
        if first == 0:
            block = gathered.at[j, loop]
            remote((block, block), block_send.at[j], block_recv.at[j, 0], {"loop": other}).start()

    def wait_blocks(j, first, last, sem):
        ref = gathered.at[j, pl.ds(first, last - first)]
        remote((ref, ref), block_send.at[j], block_recv.at[j, sem], {"loop": other}).wait_recv()

    def translate(j, first, last, high):
        def term(step):
            blocks = [gathered[j, loops * step + l] for l in range(loops)]
            columns = pl.ds(pl.multiple_of(origin(step) * pair, pair), pair)
            return dot_nt(jnp.concatenate(blocks, axis=1), both[0:high, columns])

        if last - first <= 8:
            return sum((term(step) for step in range(first + 1, last)), term(first))
        start = jnp.zeros((padded, high), jnp.float32)
        return lax.fori_loop(first, last, lambda step, total: total + term(step), start)

    pl.semaphore_wait(barrier, loops * wides - 1)
    field_copy(0).start()
    send_blocks(0, half, wides)
    send_blocks(0, 0, half)

    loads[3].wait()
    inner = dot_nt(source_all[...], eval_all[...])
    inner_high = inner.astype(jnp.bfloat16)
    inner_low = (inner - inner_high.astype(jnp.float32)).astype(jnp.bfloat16)
    length = both.shape[1]
    tile = min(length, 2048)
    for start in range(0, length, tile):
        some = both[0:width, start : start + tile]
        both[width:, start : start + tile] = (
            jnp.dot(inner_high, some, preferred_element_type=jnp.float32)
            + jnp.dot(inner_low, some, preferred_element_type=jnp.float32)
        ).astype(jnp.bfloat16)
    loads[2].wait()

    for j in range(APPLIES):
        final = j + 1 == APPLIES
        field = fields[j]
        field_copy(j).wait_recv()
        for p in range(count):
            total = None
            for n in range(near_count):
                term = dot_nt(field[sources[p, n]], near_vmem[p, n])
                total = term if total is None else total + term
            near_sum[p] = total
        if not final:
            own = jnp.concatenate(
                [near_sum[p].astype(jnp.bfloat16) for p in range(count)], axis=1
            )
            near_coeffs = dot_nt(own, source_all[...])

        high = width if final else 2 * width
        wait_blocks(j, 1, loops * half, 0)
        total = translate(j, 0, half, high)
        if wides > half:
            wait_blocks(j, loops * half, loops * wides, 1)
            total = total + translate(j, half, wides, high)
        if not final:
            gathered[j + 1, loop] = (near_coeffs + total[:, width:]).astype(jnp.bfloat16)
            send_blocks(j + 1, half, wides)
        expansion = total[:, :width].astype(jnp.bfloat16)
        for p in range(count):
            far = jnp.dot(
                expansion, eval_all[:, p * elements : (p + 1) * elements],
                preferred_element_type=jnp.float32,
            )
            value = (near_sum[p] + far).astype(jnp.bfloat16)
            if not final:
                fields[j + 1][mine + p] = value
            out[j, :, p * elements : (p + 1) * elements] = value[:rows]
        if not final:
            field_copy(j + 1).start()
            send_blocks(j + 1, 0, half)

    for j in range(APPLIES):
        field_copy(j).wait_send()
        most = gathered.at[j, pl.ds(0, loops * wides - 1)]
        remote((most, most), block_send.at[j], block_recv.at[j, 0], {"loop": other}).wait_send()


def per_device(
    density, near_blocks, near_source, source_basis, cluster_of, translation, eval_basis
):
    wides, loops = lax.axis_size("wide"), lax.axis_size("loop")
    rows, size = density.shape
    count, near_count, elements, _ = near_blocks.shape
    rank = source_basis.shape[1]
    width = CL_DEV * rank
    padded = -(-rows // 16) * 16
    vmem = pl.BlockSpec(memory_space=pltpu.VMEM)
    anywhere = pl.BlockSpec(memory_space=pl.ANY)
    low, full = jnp.bfloat16, jnp.float32
    return pl.pallas_call(
        functools.partial(kernel, wides, loops, count),
        out_shape=jax.ShapeDtypeStruct((APPLIES, rows, size), low),
        in_specs=[anywhere] * 7,
        out_specs=vmem,
        scratch_shapes=[pltpu.VMEM((loops * count, padded, elements), low)] * APPLIES
        + [
            pltpu.VMEM((APPLIES, loops * wides, padded, width), low),
            pltpu.VMEM(near_blocks.shape, low),
            pltpu.VMEM(source_basis.shape, low),
            pltpu.VMEM((2 * width, translation.shape[1]), low),
            pltpu.VMEM(eval_basis.shape, low),
            pltpu.VMEM(density.shape, low),
            pltpu.SMEM(cluster_of.shape, jnp.int32),
            pltpu.SMEM(near_source.shape, jnp.int32),
            pltpu.VMEM((width, size), low),
            pltpu.VMEM((width, size), low),
            pltpu.VMEM((count, padded, elements), full),
            pltpu.SemaphoreType.DMA((7,)),
            pltpu.SemaphoreType.DMA((APPLIES,)),
            pltpu.SemaphoreType.DMA((APPLIES,)),
            pltpu.SemaphoreType.DMA((APPLIES,)),
            pltpu.SemaphoreType.DMA((APPLIES, 2)),
        ],
        compiler_params=pltpu.CompilerParams(
            collective_id=0, has_side_effects=True, vmem_limit_bytes=60 * 2**20
        ),
        name="apply_operator",
    )(
        cluster_of, near_source, density, near_blocks, source_basis,
        translation, eval_basis,
    )


def solution(mesh):
    split = ("parts", "wide", "loop")
    return jax.shard_map(
        per_device,
        mesh=mesh,
        in_specs=(
            P(None, split),
            P(split, None, None, None),
            P(split, None),
            P(split, None, None),
            P(split),
            P(split, None),
            P(split, None, None),
        ),
        out_specs=P(None, None, split),
        check_vma=False,
    )
```

```python
import functools

import jax
import jax.numpy as jnp
from jax import lax
from jax.experimental import pallas as pl
from jax.experimental.pallas import tpu as pltpu
from jax.sharding import PartitionSpec as P

CL_DEV = 2
APPLIES = 4
MESH = pl.DeviceIdType.MESH
NT = (((1,), (1,)), ((), ()))


def dot_nt(a, b):
    return lax.dot_general(a, b, NT, preferred_element_type=jnp.float32)


def kernel(
    wides, loops, count,
    clusters_hbm, sources_hbm, density_hbm, near_hbm, source_hbm, translation_hbm, eval_hbm,
    out,
    field0, field1, field2, field3, gathered, near_vmem, source_vmem, both,
    eval_vmem, density, clusters, sources, source_all, eval_all, near_sum,
    load_sem, field_send, field_recv, block_send, near_recv, far_recv, pass_send, pass_recv,
):
    fields = (field0, field1, field2, field3)
    wide = lax.axis_index("wide")
    loop = lax.axis_index("loop")
    other = 1 - loop
    rows = density.shape[0]
    padded, elements = field0.shape[1:]
    near_count = sources.shape[1]
    rank = source_hbm.shape[1]
    width = CL_DEV * rank
    pair = loops * width
    close = max(wides // 4, 1)
    paired = wides & (wides - 1) == 0

    def partner(step):
        flipped, bit = 0, 1
        while bit < wides:
            mine_bit, step_bit = wide // bit % 2, step // bit % 2
            flipped = flipped + bit * (mine_bit + step_bit - 2 * mine_bit * step_bit)
            bit *= 2
        return flipped

    def target(step):
        return partner(step) if paired else lax.rem(wide + step, wides)

    def origin(step):
        return partner(step) if paired else lax.rem(wide - step + wides, wides)

    def each(first, last, body):
        if last - first <= 8:
            for step in reversed(range(first, last)):
                body(step)
        else:
            lax.fori_loop(0, last - first, lambda i, carry: (body(last - 1 - i), carry)[1], 0)

    barrier = pltpu.get_barrier_semaphore()

    def greet(step):
        pl.semaphore_signal(
            barrier, inc=1, device_id={"wide": target(step)}, device_id_type=MESH
        )

    def greet_both(step):
        greet(step)
        pl.semaphore_signal(
            barrier, inc=1, device_id={"wide": target(step), "loop": other}, device_id_type=MESH
        )

    each(close, wides, greet)
    each(1, close, greet_both)
    pl.semaphore_signal(barrier, inc=1, device_id={"loop": other}, device_id_type=MESH)

    loads = [
        pltpu.make_async_copy(source_hbm, source_vmem, load_sem.at[0]),
        pltpu.make_async_copy(eval_hbm, eval_vmem, load_sem.at[1]),
        pltpu.make_async_copy(near_hbm, near_vmem, load_sem.at[2]),
        pltpu.make_async_copy(translation_hbm, both.at[pl.ds(0, width)], load_sem.at[3]),
        pltpu.make_async_copy(density_hbm, density, load_sem.at[4]),
        pltpu.make_async_copy(clusters_hbm, clusters, load_sem.at[5]),
        pltpu.make_async_copy(sources_hbm, sources, load_sem.at[6]),
    ]
    for number in (4, 0, 5, 6, 1, 3, 2):
        loads[number].start()

    mine = loop * count
    loads[4].wait()
    for p in range(count):
        field0[mine + p] = jnp.zeros((padded, elements), jnp.bfloat16)
        field0[mine + p, 0:rows, :] = density[:, p * elements : (p + 1) * elements]
    for number in (0, 5, 6, 1):
        loads[number].wait()
    for p in range(count):
        for c in range(CL_DEV):
            chosen = clusters[p] == c
            source_all[c * rank : (c + 1) * rank, p * elements : (p + 1) * elements] = jnp.where(
                chosen, source_vmem[p], jnp.zeros((rank, elements), jnp.bfloat16)
            )
            eval_all[c * rank : (c + 1) * rank, p * elements : (p + 1) * elements] = jnp.where(
                chosen, eval_vmem[p], jnp.zeros((rank, elements), jnp.bfloat16)
            )
    own = jnp.concatenate([field0[mine + p] for p in range(count)], axis=1)
    gathered[0, loop, 0] = dot_nt(own, source_all[...]).astype(jnp.bfloat16)

    def remote(ref, send, recv, device):
        return pltpu.make_async_remote_copy(
            src_ref=ref[0], dst_ref=ref[1], send_sem=send, recv_sem=recv,
            device_id=device, device_id_type=MESH,
        )

    def field_copy(j):
        part = fields[j].at[pl.ds(mine, count)]
        return remote((part, part), field_send.at[j], field_recv.at[j], {"loop": other})

    def send_far(j):
        def body(step):
            remote(
                (gathered.at[j, loop, 0], gathered.at[j, loop, step]),
                block_send.at[j], far_recv.at[j, step], {"wide": target(step)},
            ).start()

        each(close, wides, body)

    def send_near(j):
        def body(step):
            ref = (gathered.at[j, loop, 0], gathered.at[j, loop, step])
            remote(
                ref, block_send.at[j], near_recv.at[j, 0], {"wide": target(step)}
            ).start()
            remote(
                ref, block_send.at[j], near_recv.at[j, 1], {"wide": target(step), "loop": other}
            ).start()

        each(1, close, body)
        block = gathered.at[j, loop, 0]
        remote((block, block), block_send.at[j], near_recv.at[j, 1], {"loop": other}).start()

    def arrive(ref, sem):
        remote((ref, ref), block_send.at[0], sem, {"loop": other}).wait_recv()

    def pass_far(j):
        def body(step):
            block = gathered.at[j, loop, step]
            arrive(block, far_recv.at[j, step])
            remote((block, block), pass_send.at[j], pass_recv.at[j], {"loop": other}).start()

        lax.fori_loop(close, wides, lambda step, carry: (body(step), carry)[1], 0, unroll=wides <= 8)

    def columns(step, l):
        return pl.ds(pl.multiple_of(origin(step) * pair + l * width, width), width)

    def summed(first, last, term, high):
        if last - first <= 8:
            return sum((term(step) for step in range(first + 1, last)), term(first))
        start = jnp.zeros((padded, high), jnp.float32)
        return lax.fori_loop(first, last, lambda step, total: total + term(step), start)

    def translate_near(j, high):
        def term(step):
            blocks = [gathered[j, l, step] for l in range(loops)]
            some = pl.ds(pl.multiple_of(origin(step) * pair, pair), pair)
            return dot_nt(jnp.concatenate(blocks, axis=1), both[0:high, some])

        return summed(0, close, term, high)

    def translate_far(j, l, high):
        if close % 2:
            def single(step):
                return dot_nt(gathered[j, l, step], both[0:high, columns(step, l)])

            return summed(close, wides, single, high)

        def term(at):
            steps = (2 * at, 2 * at + 1)
            blocks = [gathered[j, l, step] for step in steps]
            parts = [both[0:high, columns(step, l)] for step in steps]
            return dot_nt(jnp.concatenate(blocks, axis=1), jnp.concatenate(parts, axis=1))

        return summed(close // 2, wides // 2, term, high)

    pl.semaphore_wait(barrier, wides - 1 + close)
    field_copy(0).start()
    send_far(0)
    send_near(0)

    loads[3].wait()
    inner = dot_nt(source_all[...], eval_all[...])
    inner_high = inner.astype(jnp.bfloat16)
    inner_low = (inner - inner_high.astype(jnp.float32)).astype(jnp.bfloat16)
    length = both.shape[1]
    tile = min(length, 2048)
    for start in range(0, length, tile):
        some = both[0:width, start : start + tile]
        both[width:, start : start + tile] = (
            jnp.dot(inner_high, some, preferred_element_type=jnp.float32)
            + jnp.dot(inner_low, some, preferred_element_type=jnp.float32)
        ).astype(jnp.bfloat16)
    loads[2].wait()

    for j in range(APPLIES):
        final = j + 1 == APPLIES
        field = fields[j]
        field_copy(j).wait_recv()
        for p in range(count):
            total = None
            for n in range(near_count):
                term = dot_nt(field[sources[p, n]], near_vmem[p, n])
                total = term if total is None else total + term
            near_sum[p] = total
        if not final:
            own = jnp.concatenate(
                [near_sum[p].astype(jnp.bfloat16) for p in range(count)], axis=1
            )
            near_coeffs = dot_nt(own, source_all[...])

        high = width if final else 2 * width
        if close > 1:
            arrive(gathered.at[j, loop, pl.ds(1, close - 1)], near_recv.at[j, 0])
        arrive(gathered.at[j, other, pl.ds(0, close)], near_recv.at[j, 1])
        total = translate_near(j, high)
        if wides > close:
            pass_far(j)
            total = total + translate_far(j, loop, high)
            arrive(gathered.at[j, other, pl.ds(close, wides - close)], pass_recv.at[j])
            total = total + translate_far(j, other, high)
        if not final:
            gathered[j + 1, loop, 0] = (near_coeffs + total[:, width:]).astype(jnp.bfloat16)
            send_far(j + 1)
        expansion = total[:, :width].astype(jnp.bfloat16)
        for p in range(count):
            far = jnp.dot(
                expansion, eval_all[:, p * elements : (p + 1) * elements],
                preferred_element_type=jnp.float32,
            )
            value = (near_sum[p] + far).astype(jnp.bfloat16)
            if not final:
                fields[j + 1][mine + p] = value
            out[j, :, p * elements : (p + 1) * elements] = value[:rows]
        if not final:
            field_copy(j + 1).start()
            send_near(j + 1)

    for j in range(APPLIES):
        field_copy(j).wait_send()
        sent = [
            (gathered.at[j, 0], block_send), (gathered.at[j, 0, pl.ds(0, close - 1)], block_send),
            (gathered.at[j, 0, pl.ds(0, wides - close)], pass_send),
        ]
        for ref, sem in sent:
            if ref.shape[0]:
                remote((ref, ref), sem.at[j], near_recv.at[j, 0], {"loop": other}).wait_send()


def per_device(
    density, near_blocks, near_source, source_basis, cluster_of, translation, eval_basis
):
    wides, loops = lax.axis_size("wide"), lax.axis_size("loop")
    rows, size = density.shape
    count, near_count, elements, _ = near_blocks.shape
    rank = source_basis.shape[1]
    width = CL_DEV * rank
    padded = -(-rows // 16) * 16
    vmem = pl.BlockSpec(memory_space=pltpu.VMEM)
    anywhere = pl.BlockSpec(memory_space=pl.ANY)
    low, full = jnp.bfloat16, jnp.float32
    return pl.pallas_call(
        functools.partial(kernel, wides, loops, count),
        out_shape=jax.ShapeDtypeStruct((APPLIES, rows, size), low),
        in_specs=[anywhere] * 7,
        out_specs=vmem,
        scratch_shapes=[pltpu.VMEM((loops * count, padded, elements), low)] * APPLIES
        + [
            pltpu.VMEM((APPLIES, loops, wides, padded, width), low),
            pltpu.VMEM(near_blocks.shape, low),
            pltpu.VMEM(source_basis.shape, low),
            pltpu.VMEM((2 * width, translation.shape[1]), low),
            pltpu.VMEM(eval_basis.shape, low),
            pltpu.VMEM(density.shape, low),
            pltpu.SMEM(cluster_of.shape, jnp.int32),
            pltpu.SMEM(near_source.shape, jnp.int32),
            pltpu.VMEM((width, size), low),
            pltpu.VMEM((width, size), low),
            pltpu.VMEM((count, padded, elements), full),
            pltpu.SemaphoreType.DMA((7,)),
            pltpu.SemaphoreType.DMA((APPLIES,)),
            pltpu.SemaphoreType.DMA((APPLIES,)),
            pltpu.SemaphoreType.DMA((APPLIES,)),
            pltpu.SemaphoreType.DMA((APPLIES, 2)),
            pltpu.SemaphoreType.DMA((APPLIES, wides)),
            pltpu.SemaphoreType.DMA((APPLIES,)),
            pltpu.SemaphoreType.DMA((APPLIES,)),
        ],
        compiler_params=pltpu.CompilerParams(
            collective_id=0, has_side_effects=True, vmem_limit_bytes=60 * 2**20
        ),
        name="apply_operator",
    )(
        cluster_of, near_source, density, near_blocks, source_basis,
        translation, eval_basis,
    )


def solution(mesh):
    split = ("parts", "wide", "loop")
    return jax.shard_map(
        per_device,
        mesh=mesh,
        in_specs=(
            P(None, split),
            P(split, None, None, None),
            P(split, None),
            P(split, None, None),
            P(split),
            P(split, None),
            P(split, None, None),
        ),
        out_specs=P(None, None, split),
        check_vma=False,
    )
```

```python
import functools

import jax
import jax.numpy as jnp
from jax import lax
from jax.experimental import pallas as pl
from jax.experimental.pallas import tpu as pltpu
from jax.sharding import PartitionSpec as P

CL_DEV = 2
APPLIES = 4
MESH = pl.DeviceIdType.MESH
NT = (((1,), (1,)), ((), ()))


def dot_nt(a, b):
    return lax.dot_general(a, b, NT, preferred_element_type=jnp.float32)


def kernel(
    wides, loops, count,
    clusters_hbm, sources_hbm, density_hbm, near_hbm, source_hbm, translation_hbm, eval_hbm,
    out_hbm,
    field0, field1, field2, field3, gathered, near_vmem, source_vmem, both,
    eval_vmem, density, clusters, sources, source_all, eval_all, near_sum, out,
    load_sem, store_sem, field_send, field_recv, block_send, near_recv, far_recv, pass_send, pass_recv,
):
    fields = (field0, field1, field2, field3)
    wide = lax.axis_index("wide")
    loop = lax.axis_index("loop")
    other = 1 - loop
    rows = density.shape[0]
    padded, elements = field0.shape[1:]
    near_count = sources.shape[1]
    rank = source_hbm.shape[1]
    width = CL_DEV * rank
    pair = loops * width
    close = max(wides // 4, 1)
    paired = wides & (wides - 1) == 0

    def partner(step):
        flipped, bit = 0, 1
        while bit < wides:
            mine_bit, step_bit = wide // bit % 2, step // bit % 2
            flipped = flipped + bit * (mine_bit + step_bit - 2 * mine_bit * step_bit)
            bit *= 2
        return flipped

    def target(step):
        return partner(step) if paired else lax.rem(wide + step, wides)

    def origin(step):
        return partner(step) if paired else lax.rem(wide - step + wides, wides)

    def each(first, last, body):
        if last - first <= 8:
            for step in reversed(range(first, last)):
                body(step)
        else:
            lax.fori_loop(0, last - first, lambda i, carry: (body(last - 1 - i), carry)[1], 0)

    barrier = pltpu.get_barrier_semaphore()

    def greet(step):
        pl.semaphore_signal(
            barrier, inc=1, device_id={"wide": target(step)}, device_id_type=MESH
        )

    def greet_both(step):
        greet(step)
        pl.semaphore_signal(
            barrier, inc=1, device_id={"wide": target(step), "loop": other}, device_id_type=MESH
        )

    each(close, wides, greet)
    each(1, close, greet_both)
    pl.semaphore_signal(barrier, inc=1, device_id={"loop": other}, device_id_type=MESH)

    loads = [
        pltpu.make_async_copy(source_hbm, source_vmem, load_sem.at[0]),
        pltpu.make_async_copy(eval_hbm, eval_vmem, load_sem.at[1]),
        pltpu.make_async_copy(near_hbm, near_vmem, load_sem.at[2]),
        pltpu.make_async_copy(translation_hbm, both.at[pl.ds(0, width)], load_sem.at[3]),
        pltpu.make_async_copy(density_hbm, density, load_sem.at[4]),
        pltpu.make_async_copy(clusters_hbm, clusters, load_sem.at[5]),
        pltpu.make_async_copy(sources_hbm, sources, load_sem.at[6]),
    ]
    for number in (4, 0, 5, 6, 1, 3, 2):
        loads[number].start()

    mine = loop * count
    loads[4].wait()
    for p in range(count):
        field0[mine + p] = jnp.zeros((padded, elements), jnp.bfloat16)
        field0[mine + p, 0:rows, :] = density[:, p * elements : (p + 1) * elements]
    for number in (0, 5, 6, 1):
        loads[number].wait()
    for p in range(count):
        for c in range(CL_DEV):
            chosen = clusters[p] == c
            source_all[c * rank : (c + 1) * rank, p * elements : (p + 1) * elements] = jnp.where(
                chosen, source_vmem[p], jnp.zeros((rank, elements), jnp.bfloat16)
            )
            eval_all[c * rank : (c + 1) * rank, p * elements : (p + 1) * elements] = jnp.where(
                chosen, eval_vmem[p], jnp.zeros((rank, elements), jnp.bfloat16)
            )
    own = jnp.concatenate([field0[mine + p] for p in range(count)], axis=1)
    gathered[0, loop, 0] = dot_nt(own, source_all[...]).astype(jnp.bfloat16)

    def remote(ref, send, recv, device):
        return pltpu.make_async_remote_copy(
            src_ref=ref[0], dst_ref=ref[1], send_sem=send, recv_sem=recv,
            device_id=device, device_id_type=MESH,
        )

    def field_copy(j):
        part = fields[j].at[pl.ds(mine, count)]
        return remote((part, part), field_send.at[j], field_recv.at[j], {"loop": other})

    def send_far(j):
        def body(step):
            remote(
                (gathered.at[j, loop, 0], gathered.at[j, loop, step]),
                block_send.at[j], far_recv.at[j, step], {"wide": target(step)},
            ).start()

        each(close, wides, body)

    def send_near(j):
        def body(step):
            ref = (gathered.at[j, loop, 0], gathered.at[j, loop, step])
            remote(
                ref, block_send.at[j], near_recv.at[j, 0], {"wide": target(step)}
            ).start()
            remote(
                ref, block_send.at[j], near_recv.at[j, 1], {"wide": target(step), "loop": other}
            ).start()

        each(1, close, body)
        block = gathered.at[j, loop, 0]
        remote((block, block), block_send.at[j], near_recv.at[j, 1], {"loop": other}).start()

    def arrive(ref, sem):
        remote((ref, ref), block_send.at[0], sem, {"loop": other}).wait_recv()

    def pass_far(j):
        cut = (close + wides) // 2
        for low, high in ((close, cut), (cut, wides)):
            each(low, high, lambda step: arrive(gathered.at[j, loop, step], far_recv.at[j, step]))
            block = gathered.at[j, loop, pl.ds(low, high - low)]
            remote((block, block), pass_send.at[j], pass_recv.at[j], {"loop": other}).start()

    def columns(step, l):
        return pl.ds(pl.multiple_of(origin(step) * pair + l * width, width), width)

    def summed(first, last, term, high):
        if last - first <= 8:
            return sum((term(step) for step in range(first + 1, last)), term(first))
        start = jnp.zeros((padded, high), jnp.float32)
        return lax.fori_loop(first, last, lambda step, total: total + term(step), start)

    def translate_near(j, high):
        def term(step):
            blocks = [gathered[j, l, step] for l in range(loops)]
            some = pl.ds(pl.multiple_of(origin(step) * pair, pair), pair)
            return dot_nt(jnp.concatenate(blocks, axis=1), both[0:high, some])

        return summed(0, close, term, high)

    def translate_far(j, l, high):
        if close % 2:
            def single(step):
                return dot_nt(gathered[j, l, step], both[0:high, columns(step, l)])

            return summed(close, wides, single, high)

        def term(at):
            steps = (2 * at, 2 * at + 1)
            blocks = [gathered[j, l, step] for step in steps]
            parts = [both[0:high, columns(step, l)] for step in steps]
            return dot_nt(jnp.concatenate(blocks, axis=1), jnp.concatenate(parts, axis=1))

        return summed(close // 2, wides // 2, term, high)

    pl.semaphore_wait(barrier, wides - 1 + close)
    send_far(0)
    field_copy(0).start()
    send_near(0)

    loads[3].wait()
    inner = dot_nt(source_all[...], eval_all[...])
    inner_high = inner.astype(jnp.bfloat16)
    inner_low = (inner - inner_high.astype(jnp.float32)).astype(jnp.bfloat16)
    length = both.shape[1]
    tile = min(length, 2048)
    for start in range(0, length, tile):
        some = both[0:width, start : start + tile]
        both[width:, start : start + tile] = (
            jnp.dot(inner_high, some, preferred_element_type=jnp.float32)
            + jnp.dot(inner_low, some, preferred_element_type=jnp.float32)
        ).astype(jnp.bfloat16)
    loads[2].wait()

    stores = [
        pltpu.make_async_copy(out.at[j], out_hbm.at[j], store_sem.at[j]) for j in range(APPLIES)
    ]
    for j in range(APPLIES):
        final = j + 1 == APPLIES
        field = fields[j]
        field_copy(j).wait_recv()
        for p in range(count):
            total = None
            for n in range(near_count):
                term = dot_nt(field[sources[p, n]], near_vmem[p, n])
                total = term if total is None else total + term
            near_sum[p] = total
        if not final:
            own = jnp.concatenate(
                [near_sum[p].astype(jnp.bfloat16) for p in range(count)], axis=1
            )
            near_coeffs = dot_nt(own, source_all[...])

        high = width if final else 2 * width
        if close > 1:
            arrive(gathered.at[j, loop, pl.ds(1, close - 1)], near_recv.at[j, 0])
        arrive(gathered.at[j, other, pl.ds(0, close)], near_recv.at[j, 1])
        total = translate_near(j, high)
        if wides > close:
            pass_far(j)
            total = total + translate_far(j, loop, high)
            arrive(gathered.at[j, other, pl.ds(close, wides - close)], pass_recv.at[j])
            total = total + translate_far(j, other, high)
        if not final:
            gathered[j + 1, loop, 0] = (near_coeffs + total[:, width:]).astype(jnp.bfloat16)
            send_far(j + 1)
        expansion = total[:, :width].astype(jnp.bfloat16)
        for p in range(count):
            far = jnp.dot(
                expansion, eval_all[:, p * elements : (p + 1) * elements],
                preferred_element_type=jnp.float32,
            )
            value = (near_sum[p] + far).astype(jnp.bfloat16)
            if not final:
                fields[j + 1][mine + p] = value
            out[j, :, p * elements : (p + 1) * elements] = value[:rows]
        stores[j].start()
        if not final:
            field_copy(j + 1).start()
            send_near(j + 1)

    for j in range(APPLIES):
        stores[j].wait()
        field_copy(j).wait_send()
        sent = [
            (gathered.at[j, 0], block_send), (gathered.at[j, 0, pl.ds(0, close - 1)], block_send),
            (gathered.at[j, 0, pl.ds(0, wides - close)], pass_send),
        ]
        for ref, sem in sent:
            if ref.shape[0]:
                remote((ref, ref), sem.at[j], near_recv.at[j, 0], {"loop": other}).wait_send()


def per_device(
    density, near_blocks, near_source, source_basis, cluster_of, translation, eval_basis
):
    wides, loops = lax.axis_size("wide"), lax.axis_size("loop")
    rows, size = density.shape
    count, near_count, elements, _ = near_blocks.shape
    rank = source_basis.shape[1]
    width = CL_DEV * rank
    padded = -(-rows // 16) * 16
    anywhere = pl.BlockSpec(memory_space=pl.ANY)
    low, full = jnp.bfloat16, jnp.float32
    return pl.pallas_call(
        functools.partial(kernel, wides, loops, count),
        out_shape=jax.ShapeDtypeStruct((APPLIES, rows, size), low),
        in_specs=[anywhere] * 7,
        out_specs=anywhere,
        scratch_shapes=[pltpu.VMEM((loops * count, padded, elements), low)] * APPLIES
        + [
            pltpu.VMEM((APPLIES, loops, wides, padded, width), low),
            pltpu.VMEM(near_blocks.shape, low),
            pltpu.VMEM(source_basis.shape, low),
            pltpu.VMEM((2 * width, translation.shape[1]), low),
            pltpu.VMEM(eval_basis.shape, low),
            pltpu.VMEM(density.shape, low),
            pltpu.SMEM(cluster_of.shape, jnp.int32),
            pltpu.SMEM(near_source.shape, jnp.int32),
            pltpu.VMEM((width, size), low),
            pltpu.VMEM((width, size), low),
            pltpu.VMEM((count, padded, elements), full),
            pltpu.VMEM((APPLIES, rows, size), low),
            pltpu.SemaphoreType.DMA((7,)),
            pltpu.SemaphoreType.DMA((APPLIES,)),
            pltpu.SemaphoreType.DMA((APPLIES,)),
            pltpu.SemaphoreType.DMA((APPLIES,)),
            pltpu.SemaphoreType.DMA((APPLIES,)),
            pltpu.SemaphoreType.DMA((APPLIES, 2)),
            pltpu.SemaphoreType.DMA((APPLIES, wides)),
            pltpu.SemaphoreType.DMA((APPLIES,)),
            pltpu.SemaphoreType.DMA((APPLIES,)),
        ],
        compiler_params=pltpu.CompilerParams(
            collective_id=0, has_side_effects=True, vmem_limit_bytes=60 * 2**20
        ),
        name="apply_operator",
    )(
        cluster_of, near_source, density, near_blocks, source_basis,
        translation, eval_basis,
    )


def solution(mesh):
    split = ("parts", "wide", "loop")
    return jax.shard_map(
        per_device,
        mesh=mesh,
        in_specs=(
            P(None, split),
            P(split, None, None, None),
            P(split, None),
            P(split, None, None),
            P(split),
            P(split, None),
            P(split, None, None),
        ),
        out_specs=P(None, None, split),
        check_vma=False,
    )
```
